32 devices in a mesh: expert: 16 (over z, y, x), tensor: 2 (over core).
Axes of the slice: x: 2, y: 2, z: 4, core: 2. Of those that a mesh axis runs over, the one named last changes fastest.
Arguments:
- tokens: bfloat16 [512, 7168], P('expert', 'tensor'), may hold values from -6 to 6
- expert_ids: int32 [512, 8], P('expert'), may hold values from 0 to 15, all different within a row; in each aligned block of 32 rows (0 to 31, 32 to 63, ...) at most 32 rows name the same one
- combine: float32 [512, 8], P('expert'), may hold values from 0.1 to 0.5
- w_in: bfloat16 [16, 7168, 2048], P('expert', None, 'tensor'), may hold values from -0.0625 to 0.0625
- w_down: bfloat16 [16, 1024, 7168], P('expert', None, 'tensor'), may hold values from -0.1875 to 0.1875
Outputs:
- moe_out: bfloat16 [512, 7168], P('expert', 'tensor')
The draws below stay inside these ranges and needn't reach their ends.
Inputs may be any that keep to these rules, and one draw needn't show every extreme that they name: `expert_ids`: each row names 8 different experts. Within the 32 tokens of one index of expert, no expert is named by more than 32 rows.
All inputs are finite; a program needn't handle non-finite values.
Results may differ from the reference program's by a relative error of at most 0.008.
Values may be sent and summed in bfloat16 or wider, within the bound.
A program may use at most 64 MiB of HBM per device.

```python
import math
import jax
import jax.numpy as jnp
import numpy as np
from jax import lax

D = 7168
HID = 1024
TOP = 8
TOK_G = 32
EXPERTS = 16
TOKENS = 512
CAP = 32
N_EXPERT = 16
N_TENSOR = 2


def shard_levels(stream_key, shape, split, smallest, largest):
    factor_of = 1.0
    for dim, blocks in split:
        draws = jax.random.uniform(jax.random.fold_in(jax.random.fold_in(stream_key, 6), dim), (blocks,), jnp.float32, smallest / len(split), largest / len(split))
        factor_of = factor_of * jnp.repeat(jnp.exp(draws), shape[dim] // blocks).reshape((-1,) + (1,) * (len(shape) - 1 - dim))
    return factor_of


def assign_block(own_key, own, number, rows, count, top, most, slope):
    order = jax.random.permutation(own_key, count)
    packed, ordinary = shares(count, rows * top, most, slope, True), shares(count, rows * top, most, slope, False)
    places = jnp.arange(count)

    def named(sizes, turn):
        used = int((sizes > 0).sum())
        fixed = max(1, used // 4)
        passed = fixed + (places - fixed + turn * (used - fixed)) % max(1, count - fixed)
        return jnp.zeros((count,), jnp.int32).at[order[jnp.where(places < fixed, places, passed)]].set(jnp.asarray(sizes, jnp.int32))

    sizes = jnp.where(number % 4 == 0, named(packed, number // 4), named(ordinary, number - number // 4 - 1))
    mixed = jax.random.permutation(jax.random.fold_in(own, 3), count)
    source_of, sink = mixed[0:count // 2 * 2:2], mixed[1:count // 2 * 2:2]
    room = jnp.minimum(sizes[source_of] - 1, most - sizes[sink]) // 2
    room = jnp.where((source_of == order[0]) | (sink == order[0]) | (sizes[sink] == 0), 0, jnp.maximum(room, 0))
    passed = jax.random.randint(jax.random.fold_in(own, 4), (count // 2,), 0, 1 << 20) % (room + 1)
    sizes = sizes.at[source_of].add(-passed).at[sink].add(passed)
    items = jnp.searchsorted(jnp.cumsum(sizes), jnp.arange(rows * top), side="right").astype(jnp.int32)
    grid = items.reshape(top, rows).T
    grid = grid[jax.random.permutation(jax.random.fold_in(own, 1), rows)]
    turn = jax.random.randint(jax.random.fold_in(own, 2), (rows, 1), 0, top)
    return jnp.take_along_axis(grid, (jnp.arange(top)[None, :] + turn) % top, axis=1)


def shares(count, total, reach, lean, full):
    weights = [(1 << 20) // math.isqrt(standing ** lean) + 1 for standing in range(1, count + 1)]
    largest = reach if full else min(reach, max(-(-total // count), total * weights[0] // sum(weights)))
    least = 1 if total - largest >= count - 1 else 0
    counts, surplus = [largest] + [least] * (count - 1), total - largest - least * (count - 1)
    while surplus > 0:
        movable = [i for i in range(1, count) if counts[i] < largest] or [i for i in range(1, count) if counts[i] < reach]
        mass, left = sum([weights[i] for i in movable]), surplus
        for i in movable:
            addition = min(reach - counts[i], max(1, left * weights[i] // mass), surplus)
            counts[i] = counts[i] + addition
            surplus = surplus - addition
    return np.array(counts)


def scatter_about(own_key, dims, spread, limit, pieces=(), kind=jnp.bfloat16):
    array = spread * jax.random.normal(own_key, dims, jnp.float32)
    if pieces:
        array = array * shard_levels(own_key, dims, pieces, -0.22, 0.18)
    return jnp.clip(array, -limit, limit).astype(kind)


def setup_inputs(seed: int = 0) -> dict:
    arg_keys = jax.random.split(jax.random.key(seed), 6)
    tokens = scatter_about(arg_keys[0], (TOKENS, D), 1.0, 6.0, ((0, 16), (1, 2)))
    expert_ids_keys = jax.random.split(jax.random.fold_in(arg_keys[1], 1), TOKENS // TOK_G)
    expert_ids_turns = jax.random.permutation(jax.random.fold_in(arg_keys[1], 3), TOKENS // TOK_G)
    expert_ids = jax.vmap(lambda own, number: assign_block(jax.random.fold_in(arg_keys[1], 2), own, number, TOK_G, EXPERTS, TOP, CAP, 2))(expert_ids_keys, expert_ids_turns).reshape((TOKENS, TOP))
    combine = jnp.clip(0.1 + 0.4 * jax.random.uniform(arg_keys[2], (TOKENS, TOP), jnp.float32) ** shard_levels(arg_keys[2], (TOKENS, TOP), ((0, 16),), -0.2, 0.2), 0.1, 0.5)
    w_in = scatter_about(arg_keys[3], (EXPERTS, D, 2 * HID), D ** -0.5, 0.0625, ((0, 16), (2, 2)))
    w_down = scatter_about(arg_keys[4], (EXPERTS, HID, D), HID ** -0.5, 0.1875, ((0, 16), (2, 2)))
    return dict(tokens=tokens, expert_ids=expert_ids, combine=combine, w_in=w_in, w_down=w_down)


def expert_apply(rows_in, gate_up_w, down_w):
    count_rows = rows_in.shape[0]
    gate_up = jnp.dot(rows_in, gate_up_w, preferred_element_type=jnp.float32)
    blocks = gate_up.reshape(count_rows, N_TENSOR, 2, HID // N_TENSOR)
    gate_part = blocks[:, :, 0, :].reshape(count_rows, HID)
    up_part = blocks[:, :, 1, :].reshape(count_rows, HID)
    hidden = (jax.nn.silu(gate_part) * up_part).astype(jnp.bfloat16)
    return jnp.dot(hidden, down_w, preferred_element_type=jnp.float32).astype(jnp.bfloat16)


def reference(tokens, expert_ids, combine, w_in, w_down):
    tok_group = TOKENS // N_EXPERT
    one_hot = (expert_ids[:, :, None] == jnp.arange(EXPERTS, dtype=jnp.int32)[None, None, :]).astype(jnp.int32)
    per_token = jnp.sum(one_hot, axis=1).reshape(N_EXPERT, tok_group, EXPERTS)
    before = (jnp.cumsum(per_token, axis=1) - per_token).reshape(TOKENS, EXPERTS)
    slot_index = jnp.take_along_axis(before, expert_ids, axis=1)
    source = (jnp.arange(TOKENS, dtype=jnp.int32) // tok_group)[:, None]
    position = source * CAP + slot_index
    buffer_rows = N_EXPERT * CAP
    flat_index = (expert_ids * buffer_rows + position).reshape(-1).astype(jnp.int32)
    token_index = jnp.repeat(jnp.arange(TOKENS, dtype=jnp.int32), TOP)
    table = jnp.full((EXPERTS * buffer_rows,), TOKENS, dtype=jnp.int32).at[flat_index].set(token_index)
    table = table.reshape(EXPERTS, buffer_rows)
    padded = jnp.concatenate([tokens, jnp.zeros((1, D), tokens.dtype)], axis=0)

    def one_expert(number):
        rows_in = padded[table[number]]
        return expert_apply(rows_in, w_in[number], w_down[number])

    outputs = lax.map(one_expert, jnp.arange(EXPERTS, dtype=jnp.int32))
    picked = outputs.reshape(EXPERTS * buffer_rows, D)[flat_index].reshape(TOKENS, TOP, D)
    summed = jnp.einsum("tk,tkd->td", combine.astype(jnp.float32), picked.astype(jnp.float32))
    return summed.astype(jnp.bfloat16)
```

```python
import functools
import jax
import jax.numpy as jnp
from jax import lax
from jax.experimental import pallas as pl
from jax.experimental.pallas import tpu as pltpu
from jax.sharding import PartitionSpec as P

BF16 = jnp.bfloat16
F32 = jnp.float32


def tile_of(width, most):
    return next(t for t in (most, 256, 128) if width % t == 0)


def line_order(line):
    return sorted(range(1, line), key=lambda d: abs(2 * d - line)) + [0]


def layer_kernel(
    line, tokens, ids, weights, w_in, w_down, out,
    x, w1, w2, acc, hid, y, from_b, to_a, from_a, to_z, from_z,
    w_sem, z_send, a_send, b_send, t_send, x_recv, t_recv, h_send, h_recv,
    rb_send, rb_recv, ra_send, ra_recv, rz_send, rz_recv,
):
    me = lax.axis_index("expert")
    t = lax.axis_index("tensor")
    other = 1 - t
    experts = 4 * line
    rows, feat = tokens.shape
    half = hid.shape[3]
    depth = 2 * feat
    col_x, col_y, col_z = me % 2, (me // 2) % 2, me // 4
    peer_x = me + 1 - 2 * col_x
    peer_y = me + 2 - 4 * col_y
    peer_a = peer_x + t * (peer_y - peer_x)
    peer_b = peer_y + t * (peer_x - peer_y)
    quarter_a, quarter_b = 1 + t, 2 - t

    def peer_z(d):
        return ((col_z + d) % line) * 4 + col_y * 2 + col_x

    w_copies = [
        pltpu.make_async_copy(w_in.at[0, pl.ds(pl.multiple_of(k * feat, 128), feat)],
                              w1.at[pl.ds(pl.multiple_of(k * feat, 128), feat)], w_sem.at[i])
        for i, k in enumerate((t, other))
    ] + [pltpu.make_async_copy(w_down.at[0], w2, w_sem.at[2])]
    for c in w_copies:
        c.start()

    barrier = pltpu.get_barrier_semaphore()
    partners = [(peer_z(d), t) for d in range(1, line)] + [(peer_x, t), (peer_y, t), (me, other)]
    for p in partners:
        pl.semaphore_signal(barrier, inc=1, device_id=p, device_id_type=pl.DeviceIdType.MESH)

    x[t, 0, :, :feat] = tokens[...]
    lane = lax.broadcasted_iota(jnp.int32, (rows, 128), 1)
    table = jnp.zeros((rows, 128), F32)
    for k in range(ids.shape[1]):
        table += jnp.where(lane % experts == ids[:, k:k + 1], weights[:, k:k + 1], 0.0)
    high = table.astype(BF16)
    rest = table - high.astype(F32)
    mid = rest.astype(BF16)
    low = (rest - mid.astype(F32)).astype(BF16)
    part = jnp.where(lane < experts, high.astype(F32),
                     jnp.where(lane < 2 * experts, mid.astype(F32), low.astype(F32)))
    x[t, 0, :, feat:] = jnp.where(lane < 3 * experts, part, 0.0).astype(BF16)

    pl.semaphore_wait(barrier, len(partners))

    def remote(src, dst, send, recv, to):
        return pltpu.make_async_remote_copy(
            src_ref=src, dst_ref=dst, send_sem=send, recv_sem=recv,
            device_id=to, device_id_type=pl.DeviceIdType.MESH)

    def number(db, da, dz):
        return (2 * db + da) * line + dz

    def slot(db, da, dz):
        return (db * quarter_b + da * quarter_a) * line + dz

    def slot_other(db, da, dz):
        return (db * quarter_a + da * quarter_b) * line + dz

    order = line_order(line)
    sent = []

    def send(*args):
        c = remote(*args)
        c.start()
        sent.append(c)

    def forward(db, da, dz):
        src = x.at[t, slot(db, da, dz)]
        if (db, da, dz) == (0, 0, 0):
            for d in order[:-1]:
                send(src, x.at[t, line - d], z_send.at[d - 1], x_recv.at[line - d], (peer_z(d), t))
        if db == 0 and da == 0:
            send(src, x.at[t, slot(0, 1, dz)], a_send.at[dz], x_recv.at[number(0, 1, dz)], (peer_a, t))
        if db == 0:
            send(src, x.at[t, slot(1, da, dz)], b_send.at[number(0, da, dz)],
                 x_recv.at[number(1, da, dz)], (peer_b, t))
        n = number(db, da, dz)
        send(src, src, t_send.at[n], t_recv.at[n], (me, other))

    def arrive(db, da, dz):
        n = number(db, da, dz)
        dst = x.at[t, slot(db, da, dz)]
        remote(dst, dst, t_send.at[n], x_recv.at[n], (me, other)).wait_recv()

    def arrive_other(db, da, dz):
        n = number(db, da, dz)
        dst = x.at[other, slot_other(db, da, dz)]
        remote(dst, dst, t_send.at[n], t_recv.at[n], (me, other)).wait_recv()

    forward(0, 0, 0)
    acc[...] = jnp.zeros_like(acc)
    arrive(0, 1, 0)
    forward(0, 1, 0)
    for d in order[:-1]:
        dz = line - d
        arrive(0, 0, dz)
        forward(0, 0, dz)
        arrive(0, 1, dz)
        forward(0, 1, dz)

    wide = tile_of(2 * half, 256)
    group = line * rows

    def project(tt, q0, q1):
        def step(n, _):
            cols = pl.ds(pl.multiple_of(n * wide, wide), wide)
            block = jnp.concatenate(
                [x[tt, pl.ds(q * line, line), :, :feat].reshape(group, feat) for q in (q0, q1)], axis=0)
            r = jnp.dot(block, w1[pl.ds(pl.multiple_of(tt * feat, 128), feat), cols],
                        preferred_element_type=F32)
            acc[q0, :, cols] += r[:group]
            acc[q1, :, cols] += r[group:]
            return 0

        lax.fori_loop(0, 2 * half // wide, step, 0)

    def hidden(i, q):
        extra = x[t, pl.ds(q * line, line), :, feat:].reshape(group, 128).astype(F32)
        lanes = lax.broadcasted_iota(jnp.int32, (group, 128), 1)
        scale = jnp.sum(jnp.where(lanes % experts == me, extra, 0.0), axis=1, keepdims=True)
        gate = acc[q, :, :half]
        hid[t, q] = (gate / (1.0 + jnp.exp(-gate)) * acc[q, :, half:] * scale).astype(BF16)
        send(hid.at[t, q], hid.at[t, q], h_send.at[i], h_recv.at[i], (me, other))

    def hidden_other(i, q):
        remote(hid.at[other, q], hid.at[other, q], h_send.at[i], h_recv.at[i], (me, other)).wait_recv()

    w_copies[0].wait()
    project(t, 0, quarter_a)
    for dz in range(line):
        for da in range(2):
            arrive_other(0, da, dz)
    w_copies[1].wait()
    project(other, 0, quarter_b)
    hidden(0, 0)
    for dz in [0] + [line - d for d in order[:-1]]:
        for da in range(2):
            arrive(1, da, dz)
            forward(1, da, dz)
    project(t, quarter_b, 3)
    hidden(1, quarter_b)
    for dz in range(line):
        for da in range(2):
            arrive_other(1, da, dz)
    project(other, quarter_a, 3)
    hidden(2, 3)
    hidden(3, quarter_a)

    w_copies[2].wait()
    broad = tile_of(feat, 512)

    def down(q0, q1):
        def step(n, _):
            cols = pl.ds(pl.multiple_of(n * broad, broad), broad)
            block = jnp.concatenate(
                [jnp.concatenate([hid[0, q], hid[1, q]], axis=1) for q in (q0, q1)], axis=0)
            r = jnp.dot(block, w2[:, cols], preferred_element_type=F32).astype(BF16)
            y[pl.ds(q0 * line, line), :, cols] = r[:group].reshape(line, rows, broad)
            y[pl.ds(q1 * line, line), :, cols] = r[group:].reshape(line, rows, broad)
            return 0

        lax.fori_loop(0, feat // broad, step, 0)

    hidden_other(2, 3)
    hidden_other(3, quarter_b)
    down(quarter_b, 3)
    for dz in order:
        for da in (1, 0):
            n = number(0, da, dz)
            send(y.at[slot(1, da, dz)], from_b.at[n], rb_send.at[n], rb_recv.at[n], (peer_b, t))
    hidden_other(0, 0)
    hidden_other(1, quarter_a)
    down(quarter_a, 0)

    def got_b(da, dz):
        n = number(0, da, dz)
        remote(from_b.at[n], from_b.at[n], rb_send.at[n], rb_recv.at[n], (peer_b, t)).wait_recv()

    def got_a(dz):
        remote(from_a.at[dz], from_a.at[dz], ra_send.at[dz], ra_recv.at[dz], (peer_a, t)).wait_recv()

    def pass_a(dz):
        got_b(1, dz)
        to_a[dz] = (y[slot(0, 1, dz)].astype(F32) + from_b[number(0, 1, dz)].astype(F32)).astype(BF16)
        send(to_a.at[dz], from_a.at[dz], ra_send.at[dz], ra_recv.at[dz], (peer_a, t))

    def total(dz):
        got_b(0, dz)
        got_a(dz)
        return y[slot(0, 0, dz)].astype(F32) + from_b[number(0, 0, dz)].astype(F32) + from_a[dz].astype(F32)

    def pass_z(dz):
        to_z[dz - 1] = total(dz).astype(BF16)
        send(to_z.at[dz - 1], from_z.at[dz - 1], rz_send.at[dz - 1], rz_recv.at[dz - 1], (peer_z(dz), t))

    pass_a(order[0])
    for now, later in zip(order, order[1:]):
        pass_a(later)
        pass_z(now)
    result = total(0)
    for d in order[:-1]:
        remote(from_z.at[d - 1], from_z.at[d - 1], rz_send.at[d - 1], rz_recv.at[d - 1],
               (peer_z(d), t)).wait_recv()
        result = result + from_z[d - 1].astype(F32)
    out[...] = result.astype(BF16)
    for c in sent:
        c.wait_send()


def fused(tokens, expert_ids, combine, w_in, w_down):
    line = lax.axis_size("expert") // 4
    rows, feat = tokens.shape
    half = w_in.shape[2] // 2
    dma = pltpu.SemaphoreType.DMA
    block = (rows, feat)
    vmem = pl.BlockSpec(memory_space=pltpu.VMEM)
    hbm = pl.BlockSpec(memory_space=pl.ANY)
    return pl.pallas_call(
        functools.partial(layer_kernel, line),
        out_shape=jax.ShapeDtypeStruct(block, BF16),
        in_specs=[vmem, vmem, vmem, hbm, hbm],
        out_specs=vmem,
        scratch_shapes=[
            pltpu.VMEM((2, 4 * line, rows, feat + 128), BF16),
            pltpu.VMEM(w_in.shape[1:], BF16),
            pltpu.VMEM(w_down.shape[1:], BF16),
            pltpu.VMEM((4, line * rows, 2 * half), F32),
            pltpu.VMEM((2, 4, line * rows, half), BF16),
            pltpu.VMEM((4 * line,) + block, BF16),
            pltpu.VMEM((2 * line,) + block, BF16),
            pltpu.VMEM((line,) + block, BF16),
            pltpu.VMEM((line,) + block, BF16),
            pltpu.VMEM((line - 1,) + block, BF16),
            pltpu.VMEM((line - 1,) + block, BF16),
            dma((3,)), dma((line - 1,)), dma((line,)), dma((2 * line,)), dma((4 * line,)),
            dma((4 * line,)), dma((4 * line,)), dma((4,)), dma((4,)),
            dma((2 * line,)), dma((2 * line,)), dma((line,)), dma((line,)),
            dma((line - 1,)), dma((line - 1,)),
        ],
        compiler_params=pltpu.CompilerParams(
            collective_id=0, has_side_effects=True, vmem_limit_bytes=58 * 1024 * 1024),
    )(tokens, expert_ids, combine, w_in, w_down)


def gathered(tokens, expert_ids, combine, w_in, w_down):
    experts = lax.axis_size("expert")
    me = lax.axis_index("expert")
    named = expert_ids[:, :, None] == jnp.arange(experts, dtype=jnp.int32)[None, None, :]
    table = jnp.sum(jnp.where(named, combine[:, :, None], 0.0), axis=1)
    table = lax.all_gather(table, "expert", axis=0, tiled=True)
    scale = lax.dynamic_slice_in_dim(table, me, 1, axis=1)
    rows = lax.all_gather(tokens, "expert", axis=0, tiled=True)
    rows = lax.all_gather(rows, "tensor", axis=1, tiled=True)
    gate_up = jnp.dot(rows, w_in[0], preferred_element_type=F32)
    half = w_in.shape[2] // 2
    hidden = (jax.nn.silu(gate_up[:, :half]) * gate_up[:, half:]).astype(BF16)
    hidden = lax.all_gather(hidden, "tensor", axis=1, tiled=True)
    out = jnp.dot(hidden, w_down[0], preferred_element_type=F32)
    return lax.psum_scatter((out * scale).astype(BF16), "expert", scatter_dimension=0, tiled=True)


def solution(mesh):
    experts, cores = mesh.shape["expert"], mesh.shape["tensor"]

    def per_device(tokens, expert_ids, combine, w_in, w_down):
        rows, feat = tokens.shape
        fits = (cores == 2 and experts % 4 == 0 and experts >= 8 and 3 * experts <= 128
                and w_in.shape[0] == 1 and rows % 16 == 0 and feat % 128 == 0
                and w_in.shape[2] % 256 == 0)
        run = fused if fits else gathered
        return run(tokens, expert_ids, combine, w_in, w_down)

    in_specs = (
        P("expert", "tensor"),
        P("expert", None),
        P("expert", None),
        P("expert", None, "tensor"),
        P("expert", None, "tensor"),
    )
    return jax.shard_map(
        per_device, mesh=mesh, in_specs=in_specs, out_specs=P("expert", "tensor"), check_vma=False
    )
```

```python
import functools
import jax
import jax.numpy as jnp
from jax import lax
from jax.experimental import pallas as pl
from jax.experimental.pallas import tpu as pltpu
from jax.sharding import PartitionSpec as P

BF16 = jnp.bfloat16
F32 = jnp.float32


def tile_of(width, most):
    return next(t for t in (most, 256, 128) if width % t == 0)


def line_order(line):
    return sorted(range(1, line), key=lambda d: abs(2 * d - line)) + [0]


def layer_kernel(
    line, tokens, ids, weights, w_in, w_down, out,
    x, w1, w2, acc, hid, y, from_b, to_a, from_a, to_z, from_z,
    w_sem, z_send, a_send, b_send, t_send, x_recv, t_recv, h_send, h_recv,
    rb_send, rb_recv, ra_send, ra_recv, rz_send, rz_recv,
):
    me = lax.axis_index("expert")
    t = lax.axis_index("tensor")
    other = 1 - t
    experts = 4 * line
    rows, feat = tokens.shape
    half = hid.shape[3]
    depth = 2 * feat
    col_x, col_y, col_z = me % 2, (me // 2) % 2, me // 4
    peer_x = me + 1 - 2 * col_x
    peer_y = me + 2 - 4 * col_y
    peer_a = peer_x + t * (peer_y - peer_x)
    peer_b = peer_y + t * (peer_x - peer_y)
    quarter_a, quarter_b = 1 + t, 2 - t

    def peer_z(d):
        return ((col_z + d) % line) * 4 + col_y * 2 + col_x

    w_copies = [
        pltpu.make_async_copy(w_in.at[0, pl.ds(pl.multiple_of(k * feat, 128), feat)],
                              w1.at[pl.ds(pl.multiple_of(k * feat, 128), feat)], w_sem.at[i])
        for i, k in enumerate((t, other))
    ] + [pltpu.make_async_copy(w_down.at[0], w2, w_sem.at[2])]
    for c in w_copies:
        c.start()

    barrier = pltpu.get_barrier_semaphore()
    partners = [(peer_z(d), t) for d in range(1, line)] + [(peer_x, t), (peer_y, t), (me, other)]
    for p in partners:
        pl.semaphore_signal(barrier, inc=1, device_id=p, device_id_type=pl.DeviceIdType.MESH)

    x[t, 0, :, :feat] = tokens[...]
    lane = lax.broadcasted_iota(jnp.int32, (rows, 128), 1)
    table = jnp.zeros((rows, 128), F32)
    for k in range(ids.shape[1]):
        table += jnp.where(lane % experts == ids[:, k:k + 1], weights[:, k:k + 1], 0.0)
    high = table.astype(BF16)
    rest = table - high.astype(F32)
    mid = rest.astype(BF16)
    low = (rest - mid.astype(F32)).astype(BF16)
    part = jnp.where(lane < experts, high.astype(F32),
                     jnp.where(lane < 2 * experts, mid.astype(F32), low.astype(F32)))
    x[t, 0, :, feat:] = jnp.where(lane < 3 * experts, part, 0.0).astype(BF16)

    pl.semaphore_wait(barrier, len(partners))

    def remote(src, dst, send, recv, to):
        return pltpu.make_async_remote_copy(
            src_ref=src, dst_ref=dst, send_sem=send, recv_sem=recv,
            device_id=to, device_id_type=pl.DeviceIdType.MESH)

    def number(db, da, dz):
        return (2 * db + da) * line + dz

    def slot(db, da, dz):
        return (db * quarter_b + da * quarter_a) * line + dz

    def slot_other(db, da, dz):
        return (db * quarter_a + da * quarter_b) * line + dz

    order = line_order(line)
    sent = []

    def send(*args):
        c = remote(*args)
        c.start()
        sent.append(c)

    def start(*args):
        remote(*args).start()

    def move_down(dz):
        return remote(x.at[t, dz], x.at[t, dz + 1], z_send.at[dz], x_recv.at[dz + 1],
                      (peer_z(line - 1), t))

    def move_up(dz):
        to = (dz - 1) % line
        return remote(x.at[t, dz], x.at[t, to], z_send.at[line + dz], x_recv.at[to], (peer_z(1), t))

    def line_moves(do):
        for dz in range(line - 1):
            @pl.when((col_z + dz < line) & (col_z > 0))
            def _():
                do(move_down(dz))
        for dz in [0] + list(range(2, line)):
            @pl.when((col_z + dz >= (line if dz else 0)) & (col_z < line - 1))
            def _():
                do(move_up(dz))

    def forward(db, da, dz):
        src = x.at[t, slot(db, da, dz)]
        if db == 0 and da == 0:
            if dz < line - 1:
                @pl.when((col_z + dz < line) & (col_z > 0))
                def _():
                    move_down(dz).start()
            if dz != 1:
                @pl.when((col_z + dz >= (line if dz else 0)) & (col_z < line - 1))
                def _():
                    move_up(dz).start()
        if db == 0 and da == 0:
            start(src, x.at[t, slot(0, 1, dz)], a_send.at[dz], x_recv.at[number(0, 1, dz)], (peer_a, t))
        if db == 0:
            start(src, x.at[t, slot(1, da, dz)], b_send.at[number(0, da, dz)],
                 x_recv.at[number(1, da, dz)], (peer_b, t))
        n = number(db, da, dz)
        start(src, src, t_send.at[n], t_recv.at[n], (me, other))

    def arrive(db, da, dz):
        n = number(db, da, dz)
        dst = x.at[t, slot(db, da, dz)]
        remote(dst, dst, t_send.at[n], x_recv.at[n], (me, other)).wait_recv()

    def arrive_other(db, da, dz):
        n = number(db, da, dz)
        dst = x.at[other, slot_other(db, da, dz)]
        remote(dst, dst, t_send.at[n], t_recv.at[n], (me, other)).wait_recv()

    def at_distance(k, do):
        if k == 0:
            do(0)
            return

        @pl.when(col_z + k < line)
        def _():
            do(k)

        @pl.when(col_z >= k)
        def _():
            do(line - k)

    def take(db, da):
        def do(dz):
            arrive(db, da, dz)
            forward(db, da, dz)
        return do

    forward(0, 0, 0)
    acc[...] = jnp.zeros_like(acc)
    for k in range(1, line + 1):
        if k < line:
            at_distance(k, take(0, 0))
        at_distance(k - 1, take(0, 1))

    wide = tile_of(2 * half, 256)
    group = line * rows

    def project(tt, q0, q1):
        def step(n, _):
            cols = pl.ds(pl.multiple_of(n * wide, wide), wide)
            block = jnp.concatenate(
                [x[tt, pl.ds(q * line, line), :, :feat].reshape(group, feat) for q in (q0, q1)], axis=0)
            r = jnp.dot(block, w1[pl.ds(pl.multiple_of(tt * feat, 128), feat), cols],
                        preferred_element_type=F32)
            acc[q0, :, cols] += r[:group]
            acc[q1, :, cols] += r[group:]
            return 0

        lax.fori_loop(0, 2 * half // wide, step, 0)

    def hidden(i, q):
        extra = x[t, pl.ds(q * line, line), :, feat:].reshape(group, 128).astype(F32)
        lanes = lax.broadcasted_iota(jnp.int32, (group, 128), 1)
        scale = jnp.sum(jnp.where(lanes % experts == me, extra, 0.0), axis=1, keepdims=True)
        gate = acc[q, :, :half]
        hid[t, q] = (gate / (1.0 + jnp.exp(-gate)) * acc[q, :, half:] * scale).astype(BF16)
        send(hid.at[t, q], hid.at[t, q], h_send.at[i], h_recv.at[i], (me, other))

    def hidden_other(i, q):
        remote(hid.at[other, q], hid.at[other, q], h_send.at[i], h_recv.at[i], (me, other)).wait_recv()

    w_copies[0].wait()
    project(t, 0, quarter_a)
    for dz in range(line):
        for da in range(2):
            arrive_other(0, da, dz)
    w_copies[1].wait()
    project(other, 0, quarter_b)
    hidden(0, 0)
    for k in range(line):
        at_distance(k, take(1, 0))
        at_distance(k, take(1, 1))
    project(t, quarter_b, 3)
    hidden(1, quarter_b)
    for dz in range(line):
        for da in range(2):
            arrive_other(1, da, dz)
    project(other, quarter_a, 3)
    hidden(2, 3)
    hidden(3, quarter_a)

    w_copies[2].wait()
    broad = tile_of(feat, 512)

    def down(q0, q1):
        def step(n, _):
            cols = pl.ds(pl.multiple_of(n * broad, broad), broad)
            block = jnp.concatenate(
                [jnp.concatenate([hid[0, q], hid[1, q]], axis=1) for q in (q0, q1)], axis=0)
            r = jnp.dot(block, w2[:, cols], preferred_element_type=F32).astype(BF16)
            y[pl.ds(q0 * line, line), :, cols] = r[:group].reshape(line, rows, broad)
            y[pl.ds(q1 * line, line), :, cols] = r[group:].reshape(line, rows, broad)
            return 0

        lax.fori_loop(0, feat // broad, step, 0)

    hidden_other(2, 3)
    hidden_other(3, quarter_b)
    down(quarter_b, 3)
    for dz in order:
        for da in (1, 0):
            n = number(0, da, dz)
            send(y.at[slot(1, da, dz)], from_b.at[n], rb_send.at[n], rb_recv.at[n], (peer_b, t))
    hidden_other(0, 0)
    hidden_other(1, quarter_a)
    down(quarter_a, 0)

    def got_b(da, dz):
        n = number(0, da, dz)
        remote(from_b.at[n], from_b.at[n], rb_send.at[n], rb_recv.at[n], (peer_b, t)).wait_recv()

    def got_a(dz):
        remote(from_a.at[dz], from_a.at[dz], ra_send.at[dz], ra_recv.at[dz], (peer_a, t)).wait_recv()

    def pass_a(dz):
        got_b(1, dz)
        to_a[dz] = (y[slot(0, 1, dz)].astype(F32) + from_b[number(0, 1, dz)].astype(F32)).astype(BF16)
        send(to_a.at[dz], from_a.at[dz], ra_send.at[dz], ra_recv.at[dz], (peer_a, t))

    def total(dz):
        got_b(0, dz)
        got_a(dz)
        return y[slot(0, 0, dz)].astype(F32) + from_b[number(0, 0, dz)].astype(F32) + from_a[dz].astype(F32)

    def pass_z(dz):
        to_z[dz - 1] = total(dz).astype(BF16)
        send(to_z.at[dz - 1], from_z.at[dz - 1], rz_send.at[dz - 1], rz_recv.at[dz - 1], (peer_z(dz), t))

    pass_a(order[0])
    for now, later in zip(order, order[1:]):
        pass_a(later)
        pass_z(now)
    result = total(0)
    for d in order[:-1]:
        remote(from_z.at[d - 1], from_z.at[d - 1], rz_send.at[d - 1], rz_recv.at[d - 1],
               (peer_z(d), t)).wait_recv()
        result = result + from_z[d - 1].astype(F32)
    out[...] = result.astype(BF16)
    for c in sent:
        c.wait_send()
    line_moves(lambda c: c.wait_send())
    for dz in range(line):
        for da in range(2):
            src = x.at[t, slot(0, da, dz)]
            if da == 0:
                remote(src, src, a_send.at[dz], x_recv.at[dz], (peer_a, t)).wait_send()
            n = number(0, da, dz)
            remote(src, src, b_send.at[n], x_recv.at[n], (peer_b, t)).wait_send()
            for db in range(2):
                n = number(db, da, dz)
                src = x.at[t, slot(db, da, dz)]
                remote(src, src, t_send.at[n], t_recv.at[n], (me, other)).wait_send()


def fused(tokens, expert_ids, combine, w_in, w_down):
    line = lax.axis_size("expert") // 4
    rows, feat = tokens.shape
    half = w_in.shape[2] // 2
    dma = pltpu.SemaphoreType.DMA
    block = (rows, feat)
    vmem = pl.BlockSpec(memory_space=pltpu.VMEM)
    hbm = pl.BlockSpec(memory_space=pl.ANY)
    return pl.pallas_call(
        functools.partial(layer_kernel, line),
        out_shape=jax.ShapeDtypeStruct(block, BF16),
        in_specs=[vmem, vmem, vmem, hbm, hbm],
        out_specs=vmem,
        scratch_shapes=[
            pltpu.VMEM((2, 4 * line, rows, feat + 128), BF16),
            pltpu.VMEM(w_in.shape[1:], BF16),
            pltpu.VMEM(w_down.shape[1:], BF16),
            pltpu.VMEM((4, line * rows, 2 * half), F32),
            pltpu.VMEM((2, 4, line * rows, half), BF16),
            pltpu.VMEM((4 * line,) + block, BF16),
            pltpu.VMEM((2 * line,) + block, BF16),
            pltpu.VMEM((line,) + block, BF16),
            pltpu.VMEM((line,) + block, BF16),
            pltpu.VMEM((line - 1,) + block, BF16),
            pltpu.VMEM((line - 1,) + block, BF16),
            dma((3,)), dma((2 * line,)), dma((line,)), dma((2 * line,)), dma((4 * line,)),
            dma((4 * line,)), dma((4 * line,)), dma((4,)), dma((4,)),
            dma((2 * line,)), dma((2 * line,)), dma((line,)), dma((line,)),
            dma((line - 1,)), dma((line - 1,)),
        ],
        compiler_params=pltpu.CompilerParams(
            collective_id=0, has_side_effects=True, vmem_limit_bytes=58 * 1024 * 1024),
    )(tokens, expert_ids, combine, w_in, w_down)


def gathered(tokens, expert_ids, combine, w_in, w_down):
    experts = lax.axis_size("expert")
    me = lax.axis_index("expert")
    named = expert_ids[:, :, None] == jnp.arange(experts, dtype=jnp.int32)[None, None, :]
    table = jnp.sum(jnp.where(named, combine[:, :, None], 0.0), axis=1)
    table = lax.all_gather(table, "expert", axis=0, tiled=True)
    scale = lax.dynamic_slice_in_dim(table, me, 1, axis=1)
    rows = lax.all_gather(tokens, "expert", axis=0, tiled=True)
    rows = lax.all_gather(rows, "tensor", axis=1, tiled=True)
    gate_up = jnp.dot(rows, w_in[0], preferred_element_type=F32)
    half = w_in.shape[2] // 2
    hidden = (jax.nn.silu(gate_up[:, :half]) * gate_up[:, half:]).astype(BF16)
    hidden = lax.all_gather(hidden, "tensor", axis=1, tiled=True)
    out = jnp.dot(hidden, w_down[0], preferred_element_type=F32)
    return lax.psum_scatter((out * scale).astype(BF16), "expert", scatter_dimension=0, tiled=True)


def solution(mesh):
    experts, cores = mesh.shape["expert"], mesh.shape["tensor"]

    def per_device(tokens, expert_ids, combine, w_in, w_down):
        rows, feat = tokens.shape
        fits = (cores == 2 and experts % 4 == 0 and experts >= 8 and 3 * experts <= 128
                and w_in.shape[0] == 1 and rows % 16 == 0 and feat % 128 == 0
                and w_in.shape[2] % 256 == 0)
        run = fused if fits else gathered
        return run(tokens, expert_ids, combine, w_in, w_down)

    in_specs = (
        P("expert", "tensor"),
        P("expert", None),
        P("expert", None),
        P("expert", None, "tensor"),
        P("expert", None, "tensor"),
    )
    return jax.shard_map(
        per_device, mesh=mesh, in_specs=in_specs, out_specs=P("expert", "tensor"), check_vma=False
    )
```

```python
import functools
import jax
import jax.numpy as jnp
from jax import lax
from jax.experimental import pallas as pl
from jax.experimental.pallas import tpu as pltpu
from jax.sharding import PartitionSpec as P

BF16 = jnp.bfloat16
F32 = jnp.float32


def tile_of(width, most):
    return next(t for t in (most, 256, 128) if width % t == 0)


def line_order(line):
    return sorted(range(1, line), key=lambda d: abs(2 * d - line)) + [0]


def layer_kernel(
    line, parts, tokens, routes, w_in, w_down, out,
    x, w1, w2, acc, hid, y, from_b, to_a, from_a, to_z, from_z,
    w_sem, z_send, a_send, b_send, t_send, x_recv, t_recv, h_send, h_recv,
    rb_send, rb_recv, ra_send, ra_recv, rz_send, rz_recv,
):
    me = lax.axis_index("expert")
    t = lax.axis_index("tensor")
    other = 1 - t
    experts = 4 * line
    rows, feat = tokens.shape
    piece = rows // parts
    half = hid.shape[3]
    depth = 2 * feat
    col_x, col_y, col_z = me % 2, (me // 2) % 2, me // 4
    peer_x = me + 1 - 2 * col_x
    peer_y = me + 2 - 4 * col_y
    peer_a = peer_x + t * (peer_y - peer_x)
    peer_b = peer_y + t * (peer_x - peer_y)
    quarter_a, quarter_b = 1 + t, 2 - t

    def peer_z(d):
        return ((col_z + d) % line) * 4 + col_y * 2 + col_x

    w_copies = [
        pltpu.make_async_copy(w_in.at[0, pl.ds(pl.multiple_of(k * feat, 128), feat)],
                              w1.at[pl.ds(pl.multiple_of(k * feat, 128), feat)], w_sem.at[i])
        for i, k in enumerate((t, other))
    ] + [pltpu.make_async_copy(w_down.at[0], w2, w_sem.at[2])]
    for c in w_copies:
        c.start()

    barrier = pltpu.get_barrier_semaphore()
    partners = [(peer_z(d), t) for d in range(1, line)] + [(peer_x, t), (peer_y, t), (me, other)]
    for p in partners:
        pl.semaphore_signal(barrier, inc=1, device_id=p, device_id_type=pl.DeviceIdType.MESH)

    x[t, 0, :, :feat] = tokens[...]
    lane = lax.broadcasted_iota(jnp.int32, (rows, 128), 1)
    expert_of = (lane % experts).astype(F32)
    top = routes.shape[1] // 2
    table = jnp.zeros((rows, 128), F32)
    for k in range(top):
        table += jnp.where(expert_of == routes[:, k:k + 1], routes[:, top + k:top + k + 1], 0.0)
    high = table.astype(BF16)
    rest = table - high.astype(F32)
    mid = rest.astype(BF16)
    low = (rest - mid.astype(F32)).astype(BF16)
    part = jnp.where(lane < experts, high.astype(F32),
                     jnp.where(lane < 2 * experts, mid.astype(F32), low.astype(F32)))
    x[t, 0, :, feat:] = jnp.where(lane < 3 * experts, part, 0.0).astype(BF16)

    pl.semaphore_wait(barrier, len(partners))

    def remote(src, dst, send, recv, to):
        return pltpu.make_async_remote_copy(
            src_ref=src, dst_ref=dst, send_sem=send, recv_sem=recv,
            device_id=to, device_id_type=pl.DeviceIdType.MESH)

    def number(db, da, dz):
        return (2 * db + da) * line + dz

    def slot(db, da, dz):
        return (db * quarter_b + da * quarter_a) * line + dz

    def slot_other(db, da, dz):
        return (db * quarter_a + da * quarter_b) * line + dz

    order = line_order(line)
    sent = []

    def send(*args):
        c = remote(*args)
        c.start()
        sent.append(c)

    def rows_of(h):
        return pl.ds(h * piece, piece)

    def own(db, da, dz, h):
        return x.at[t, slot(db, da, dz), rows_of(h)]

    def move_down(dz, h):
        return remote(x.at[t, dz, rows_of(h)], x.at[t, dz + 1, rows_of(h)], z_send.at[dz, h],
                      x_recv.at[dz + 1, h], (peer_z(line - 1), t))

    def move_up(dz, h):
        to = (dz - 1) % line
        return remote(x.at[t, dz, rows_of(h)], x.at[t, to, rows_of(h)], z_send.at[line + dz, h],
                      x_recv.at[to, h], (peer_z(1), t))

    def line_moves(dz, h, do):
        if dz < line - 1:
            @pl.when((col_z + dz < line) & (col_z > 0))
            def _():
                do(move_down(dz, h))
        if dz != 1:
            @pl.when((col_z + dz >= (line if dz else 0)) & (col_z < line - 1))
            def _():
                do(move_up(dz, h))

    def moves(db, da, dz, h, do):
        src = own(db, da, dz, h)
        n = number(db, da, dz)
        if db == 0 and da == 0:
            line_moves(dz, h, do)
            do(remote(src, own(0, 1, dz, h), a_send.at[dz, h], x_recv.at[number(0, 1, dz), h], (peer_a, t)))
        if db == 0:
            do(remote(src, own(1, da, dz, h), b_send.at[n, h], x_recv.at[number(1, da, dz), h], (peer_b, t)))
        do(remote(src, src, t_send.at[n, h], t_recv.at[n, h], (me, other)))

    def forward(db, da, dz, h):
        moves(db, da, dz, h, lambda c: c.start())

    def arrive(db, da, dz, h):
        n = number(db, da, dz)
        dst = own(db, da, dz, h)
        remote(dst, dst, t_send.at[n, h], x_recv.at[n, h], (me, other)).wait_recv()

    def arrive_other(db, da, dz):
        n = number(db, da, dz)
        for h in range(parts):
            dst = x.at[other, slot_other(db, da, dz), rows_of(h)]
            remote(dst, dst, t_send.at[n, h], t_recv.at[n, h], (me, other)).wait_recv()

    def at_distance(k, do):
        if k == 0:
            do(0)
            return

        @pl.when(col_z + k < line)
        def _():
            do(k)

        @pl.when(col_z >= k)
        def _():
            do(line - k)

    def take(db, da, h):
        def do(dz):
            arrive(db, da, dz, h)
            forward(db, da, dz, h)
        return do

    for h in range(parts):
        forward(0, 0, 0, h)
    acc[...] = jnp.zeros_like(acc)
    for k in range(1, line + 1):
        for h in range(parts):
            if k < line:
                at_distance(k, take(0, 0, h))
            at_distance(k - 1, take(0, 1, h))

    wide = tile_of(2 * half, 256)
    group = line * rows

    def project(tt, q0, q1):
        def step(n, _):
            cols = pl.ds(pl.multiple_of(n * wide, wide), wide)
            block = jnp.concatenate(
                [x[tt, pl.ds(q * line, line), :, :feat].reshape(group, feat) for q in (q0, q1)], axis=0)
            r = jnp.dot(block, w1[pl.ds(pl.multiple_of(tt * feat, 128), feat), cols],
                        preferred_element_type=F32)
            acc[q0, :, cols] += r[:group]
            acc[q1, :, cols] += r[group:]
            return 0

        lax.fori_loop(0, 2 * half // wide, step, 0)

    def hidden(i, q):
        extra = x[t, pl.ds(q * line, line), :, feat:].reshape(group, 128).astype(F32)
        lanes = lax.broadcasted_iota(jnp.int32, (group, 128), 1)
        scale = jnp.sum(jnp.where(lanes % experts == me, extra, 0.0), axis=1, keepdims=True)
        gate = acc[q, :, :half]
        hid[t, q] = (gate / (1.0 + jnp.exp(-gate)) * acc[q, :, half:] * scale).astype(BF16)
        send(hid.at[t, q], hid.at[t, q], h_send.at[i], h_recv.at[i], (me, other))

    def hidden_other(i, q):
        remote(hid.at[other, q], hid.at[other, q], h_send.at[i], h_recv.at[i], (me, other)).wait_recv()

    w_copies[0].wait()
    project(t, 0, quarter_a)
    for dz in range(line):
        for da in range(2):
            arrive_other(0, da, dz)
    w_copies[1].wait()
    project(other, 0, quarter_b)
    hidden(0, 0)
    for k in range(line):
        for h in range(parts):
            at_distance(k, take(1, 0, h))
            at_distance(k, take(1, 1, h))
    project(t, quarter_b, 3)
    hidden(1, quarter_b)
    for dz in range(line):
        for da in range(2):
            arrive_other(1, da, dz)
    project(other, quarter_a, 3)
    hidden(2, 3)
    hidden(3, quarter_a)

    w_copies[2].wait()
    broad = tile_of(feat, 512)

    def down(q0, q1):
        def step(n, _):
            cols = pl.ds(pl.multiple_of(n * broad, broad), broad)
            block = jnp.concatenate(
                [jnp.concatenate([hid[0, q], hid[1, q]], axis=1) for q in (q0, q1)], axis=0)
            r = jnp.dot(block, w2[:, cols], preferred_element_type=F32).astype(BF16)
            y[pl.ds(q0 * line, line), :, cols] = r[:group].reshape(line, rows, broad)
            y[pl.ds(q1 * line, line), :, cols] = r[group:].reshape(line, rows, broad)
            return 0

        lax.fori_loop(0, feat // broad, step, 0)

    hidden_other(2, 3)
    hidden_other(3, quarter_b)
    down(quarter_b, 3)
    for dz in order:
        for da in (1, 0):
            n = number(0, da, dz)
            for h in range(parts):
                send(y.at[slot(1, da, dz), rows_of(h)], from_b.at[n, rows_of(h)],
                     rb_send.at[n, h], rb_recv.at[n, h], (peer_b, t))
    hidden_other(0, 0)
    hidden_other(1, quarter_a)
    down(quarter_a, 0)

    def got(buf, send_sem, recv_sem, n, h, to):
        ref = buf.at[n, rows_of(h)]
        remote(ref, ref, send_sem.at[n, h], recv_sem.at[n, h], to).wait_recv()

    def pass_a(dz, h):
        n = number(0, 1, dz)
        got(from_b, rb_send, rb_recv, n, h, (peer_b, t))
        r = rows_of(h)
        to_a[dz, r] = (y[slot(0, 1, dz), r].astype(F32) + from_b[n, r].astype(F32)).astype(BF16)
        send(to_a.at[dz, r], from_a.at[dz, r], ra_send.at[dz, h], ra_recv.at[dz, h], (peer_a, t))

    def total(dz, h):
        got(from_b, rb_send, rb_recv, dz, h, (peer_b, t))
        got(from_a, ra_send, ra_recv, dz, h, (peer_a, t))
        r = rows_of(h)
        return y[slot(0, 0, dz), r].astype(F32) + from_b[dz, r].astype(F32) + from_a[dz, r].astype(F32)

    def pass_z(dz, h):
        r = rows_of(h)
        to_z[dz - 1, r] = total(dz, h).astype(BF16)
        send(to_z.at[dz - 1, r], from_z.at[dz - 1, r], rz_send.at[dz - 1, h], rz_recv.at[dz - 1, h],
             (peer_z(dz), t))

    for h in range(parts):
        pass_a(order[0], h)
    for now, later in zip(order, order[1:]):
        for h in range(parts):
            pass_a(later, h)
            pass_z(now, h)
    for h in range(parts):
        result = total(0, h)
        for d in order[:-1]:
            got(from_z, rz_send, rz_recv, d - 1, h, (peer_z(d), t))
            result = result + from_z[d - 1, rows_of(h)].astype(F32)
        out[rows_of(h)] = result.astype(BF16)
    for c in sent:
        c.wait_send()
    for db in range(2):
        for da in range(2):
            for dz in range(line):
                for h in range(parts):
                    moves(db, da, dz, h, lambda c: c.wait_send())


def fused(tokens, expert_ids, combine, w_in, w_down):
    line = lax.axis_size("expert") // 4
    rows, feat = tokens.shape
    half = w_in.shape[2] // 2
    routes = jnp.concatenate([expert_ids.astype(F32), combine], axis=1)
    parts = 2 if rows % 32 == 0 else 1
    dma = pltpu.SemaphoreType.DMA
    block = (rows, feat)
    vmem = pl.BlockSpec(memory_space=pltpu.VMEM)
    hbm = pl.BlockSpec(memory_space=pl.ANY)
    return pl.pallas_call(
        functools.partial(layer_kernel, line, parts),
        out_shape=jax.ShapeDtypeStruct(block, BF16),
        in_specs=[vmem, vmem, hbm, hbm],
        out_specs=vmem,
        scratch_shapes=[
            pltpu.VMEM((2, 4 * line, rows, feat + 128), BF16),
            pltpu.VMEM(w_in.shape[1:], BF16),
            pltpu.VMEM(w_down.shape[1:], BF16),
            pltpu.VMEM((4, line * rows, 2 * half), F32),
            pltpu.VMEM((2, 4, line * rows, half), BF16),
            pltpu.VMEM((4 * line,) + block, BF16),
            pltpu.VMEM((2 * line,) + block, BF16),
            pltpu.VMEM((line,) + block, BF16),
            pltpu.VMEM((line,) + block, BF16),
            pltpu.VMEM((line - 1,) + block, BF16),
            pltpu.VMEM((line - 1,) + block, BF16),
            dma((3,)), dma((2 * line, parts)), dma((line, parts)), dma((2 * line, parts)),
            dma((4 * line, parts)), dma((4 * line, parts)), dma((4 * line, parts)), dma((4,)), dma((4,)),
            dma((2 * line, parts)), dma((2 * line, parts)), dma((line, parts)), dma((line, parts)),
            dma((line - 1, parts)), dma((line - 1, parts)),
        ],
        compiler_params=pltpu.CompilerParams(
            collective_id=0, has_side_effects=True, vmem_limit_bytes=58 * 1024 * 1024),
    )(tokens, routes, w_in, w_down)


def gathered(tokens, expert_ids, combine, w_in, w_down):
    experts = lax.axis_size("expert")
    me = lax.axis_index("expert")
    named = expert_ids[:, :, None] == jnp.arange(experts, dtype=jnp.int32)[None, None, :]
    table = jnp.sum(jnp.where(named, combine[:, :, None], 0.0), axis=1)
    table = lax.all_gather(table, "expert", axis=0, tiled=True)
    scale = lax.dynamic_slice_in_dim(table, me, 1, axis=1)
    rows = lax.all_gather(tokens, "expert", axis=0, tiled=True)
    rows = lax.all_gather(rows, "tensor", axis=1, tiled=True)
    gate_up = jnp.dot(rows, w_in[0], preferred_element_type=F32)
    half = w_in.shape[2] // 2
    hidden = (jax.nn.silu(gate_up[:, :half]) * gate_up[:, half:]).astype(BF16)
    hidden = lax.all_gather(hidden, "tensor", axis=1, tiled=True)
    out = jnp.dot(hidden, w_down[0], preferred_element_type=F32)
    return lax.psum_scatter((out * scale).astype(BF16), "expert", scatter_dimension=0, tiled=True)


def solution(mesh):
    experts, cores = mesh.shape["expert"], mesh.shape["tensor"]

    def per_device(tokens, expert_ids, combine, w_in, w_down):
        rows, feat = tokens.shape
        fits = (cores == 2 and experts % 4 == 0 and experts >= 8 and 3 * experts <= 128
                and w_in.shape[0] == 1 and rows % 16 == 0 and feat % 128 == 0
                and w_in.shape[2] % 256 == 0)
        run = fused if fits else gathered
        return run(tokens, expert_ids, combine, w_in, w_down)

    in_specs = (
        P("expert", "tensor"),
        P("expert", None),
        P("expert", None),
        P("expert", None, "tensor"),
        P("expert", None, "tensor"),
    )
    return jax.shard_map(
        per_device, mesh=mesh, in_specs=in_specs, out_specs=P("expert", "tensor"), check_vma=False
    )
```
